256 devices in a mesh: pair: 32 (over y, x, core), grow: 4 (over z_hi), gcol: 2 (over z_lo).
Axes of the slice: x: 4, y: 4, z: 8 (z_hi: 4, z_lo: 2; z = z_hi * 2 + z_lo), core: 2. Of those that a mesh axis runs over, the one named last changes fastest.
Arguments:
- slab_density: bfloat16 [8192, 16], P('pair', ('grow', 'gcol')), may hold values from -0.62890625 to 0.62890625
- column_density: bfloat16 [8192, 12288], P('pair', ('gcol', 'grow')), may hold values from -0.62890625 to 0.62890625
- bin_index: int32 [8192], P('pair'), may hold values from 0 to 127
- occupation: int32 [8192], P('pair'), may hold values from -1 to 1, as said below
Outputs:
- polarization: float32 [64, 16, 12288], P(None, 'grow', ('gcol', 'pair'))
The draws below stay inside these ranges and needn't reach their ends.
Inputs may be any that keep to these rules, and one draw needn't show every extreme that they name: `occupation`: each entry is -1 or +1.
All inputs are finite; a program needn't handle non-finite values.
Results may differ from the reference program's by a relative error of at most 0.0003.
Values may be sent and summed in bfloat16 or wider, within the bound.
No kernel may reach another device: no remote copies, remote signals or barrier semaphores. Data moves between devices by JAX's collectives and lax.ppermute only.
A program may use at most 64 MiB of HBM per device.

```python
import jax
import jax.numpy as jnp
from jax import lax

GC = 12288
BINS = 128
FREQS = 64
GR = 16
PAIRS = 8192


def draw_occupation(key, part):
    key = jax.random.fold_in(key, 11)
    return (2 * jax.random.randint(key, (PAIRS,), 0, 2) - 1).astype(jnp.int32)


def set_ends(array, key, least, top_value):
    extent = array.shape
    place = [jax.random.randint(jax.random.fold_in(key, axis), (), 0, extent[axis]) for axis in range(len(extent))]
    array = array.at[tuple(place)].set(least)
    longest = extent.index(max(extent))
    place[longest] = (place[longest] + 1) % extent[longest]
    return array.at[tuple(place)].set(top_value)


def steps_of(own_key, dims, cuts, least, largest):
    factor_of = 1.0
    for dim, shards_of in cuts:
        draws = jax.random.uniform(jax.random.fold_in(jax.random.fold_in(own_key, 6), dim), (shards_of,), jnp.float32, least / len(cuts), largest / len(cuts))
        factor_of = factor_of * jnp.repeat(jnp.exp(draws), dims[dim] // shards_of).reshape((-1,) + (1,) * (len(dims) - 1 - dim))
    return factor_of


def noise(key, shape, spread, most, split=(), held_as=jnp.bfloat16):
    drawn = jax.random.normal(key, shape, jnp.float32) * spread
    if len(split) > 0:
        drawn = steps_of(key, shape, split, -0.22, 0.18) * drawn
    return jnp.clip(drawn, min=-most, max=most).astype(held_as)


def setup_inputs(seed: int = 0) -> dict:
    seeds = jax.random.split(jax.random.key(seed), 5)
    return {
        "slab_density": noise(seeds[0], (PAIRS, GR), (PAIRS ** -0.25), 0.62890625, ((0, 32), (1, 8))),
        "column_density": noise(seeds[1], (PAIRS, GC), (PAIRS ** -0.25), 0.62890625, ((0, 32), (1, 8))),
        "bin_index": set_ends(jax.random.randint(seeds[2], (PAIRS,), 0, BINS), jax.random.fold_in(seeds[2], 1), 0, BINS - 1).astype(jnp.int32),
        "occupation": draw_occupation(jax.random.fold_in(seeds[4], 71), 0),
    }


def hilbert_table():
    energies = (jnp.arange(BINS, dtype=jnp.float32) + 0.5) * (4.0 / BINS)
    real_freq = (jnp.arange(FREQS, dtype=jnp.float32) + 0.5) * (4.0 / FREQS)
    broadening = 4.0 / BINS
    below = real_freq[:, None] - energies[None, :]
    above = real_freq[:, None] + energies[None, :]
    return below / (below * below + broadening * broadening) - above / (above * above + broadening * broadening)


def reference(slab_density, column_density, bin_index, occupation):
    kernel = hilbert_table()
    occupied = (bin_index[:, None] == jnp.arange(BINS, dtype=jnp.int32)[None, :]).astype(jnp.float32)
    occupied = occupied * occupation[:, None].astype(jnp.float32)
    pair_weight = jnp.dot(occupied, kernel.T, precision=lax.Precision.HIGHEST)
    scaled_left = pair_weight[:, :, None] * slab_density.astype(jnp.float32)[:, None, :]
    scaled_left = scaled_left.reshape(PAIRS, FREQS * GR)
    result = lax.dot_general(scaled_left, column_density.astype(jnp.float32), (((0,), (0,)), ((), ())), precision=lax.Precision.HIGHEST)
    return result.reshape(FREQS, GR, GC)
```

```python
import functools

import jax
import jax.numpy as jnp
import numpy as np
from jax import lax
from jax.experimental import pallas as pl
from jax.experimental.pallas import tpu as pltpu
from jax.sharding import PartitionSpec as P

BINS = 128
FREQS = 64
GR = 16
Y = 4
X = 4
CORES = 2
Z = 4
CHIPS = Y * X
PART = 48
BF16 = jnp.bfloat16


def hilbert_table():
    one = np.float32
    energies = (np.arange(BINS, dtype=np.float32) + one(0.5)) * one(4.0 / BINS)
    real_freq = (np.arange(FREQS, dtype=np.float32) + one(0.5)) * one(4.0 / FREQS)
    broadening = one(4.0 / BINS)
    below = real_freq[:, None] - energies[None, :]
    above = real_freq[:, None] + energies[None, :]
    return below / (below * below + broadening * broadening) - above / (
        above * above + broadening * broadening
    )


def place(y, xc, z):
    return (y * X * CORES + xc) * Z + z


def polarize(table_ref, recv_ref, out_ref, hot_ref):
    pairs = recv_ref.shape[2]
    cols = CORES * PART
    bin_of_row = lax.broadcasted_iota(jnp.int32, (BINS, pairs), 0).astype(jnp.float32)
    for source in range(CHIPS):
        bins = recv_ref[source, cols + GR : cols + 2 * GR, :].astype(jnp.float32)[0:1, :]
        hot_ref[source] = jnp.where(bins == bin_of_row, 1.0, 0.0).astype(BF16)
    table = table_ref[...]
    for group in range(Z):
        total = jnp.zeros((4 * BINS, cols), jnp.float32)
        for source in range(CHIPS):
            hot = hot_ref[source]
            slab = recv_ref[source, cols : cols + GR, :]
            left = jnp.concatenate(
                [hot * slab[4 * group + i : 4 * group + i + 1, :] for i in range(4)], axis=0
            )
            total = total + lax.dot_general(
                left,
                recv_ref[source, :cols, :],
                (((1,), (1,)), ((), ())),
                preferred_element_type=jnp.float32,
            )
        for half in range(2):
            both = [
                jnp.dot(
                    table,
                    total[(2 * half + i) * BINS : (2 * half + i + 1) * BINS, :],
                    precision=lax.Precision.HIGHEST,
                    preferred_element_type=jnp.float32,
                )
                for i in range(2)
            ]
            lane = (2 * group + half) * 2 * FREQS
            out_ref[:, lane : lane + 2 * FREQS] = jnp.concatenate(both, axis=0).T


def per_device(slab_density, column_density, bin_index, occupation):
    pairs = slab_density.shape[0]
    me = lax.axis_index("pair")
    core = me % CORES
    my_y = me // (X * CORES)
    my_z = lax.axis_index("grow")

    signed = (slab_density * occupation[:, None].astype(BF16)).T
    rows = jnp.concatenate(
        [signed, lax.ppermute(signed, "gcol", [(0, 1), (1, 0)])], axis=0
    )
    gcol = lax.axis_index("gcol")
    rows = jnp.where(gcol == 0, rows, jnp.roll(rows, 2, axis=0))
    slabs = jnp.zeros((Z, 4, pairs), BF16)
    slabs = lax.dynamic_update_index_in_dim(slabs, rows, my_z, 0)
    for t in range(1, Z):
        got = lax.ppermute(rows, "grow", [(z, (z + t) % Z) for z in range(Z)])
        slabs = lax.dynamic_update_index_in_dim(slabs, got, (my_z - t) % Z, 0)
    meta = jnp.concatenate(
        [
            slabs.reshape(GR, pairs),
            jnp.broadcast_to(bin_index.astype(BF16)[None, :], (GR, pairs)),
        ],
        axis=0,
    )

    columns = column_density.T.reshape(X, CORES, Y, PART, pairs)
    columns = columns.transpose(2, 0, 1, 3, 4).reshape(CHIPS, CORES * PART, pairs)
    payload = jnp.concatenate(
        [columns, jnp.broadcast_to(meta[None], (CHIPS, 2 * GR, pairs))], axis=1
    )
    groups = [
        [(y * X + x) * CORES + c for y in range(Y) for x in range(X)] for c in range(CORES)
    ]
    received = lax.all_to_all(
        payload, "pair", 0, 0, axis_index_groups=groups, tiled=True
    )

    lanes = GR * FREQS
    part = pl.pallas_call(
        polarize,
        out_shape=jax.ShapeDtypeStruct((CORES * PART, lanes), jnp.float32),
        scratch_shapes=[pltpu.VMEM((CHIPS, BINS, pairs), BF16)],
        compiler_params=pltpu.CompilerParams(vmem_limit_bytes=40 * 1024 * 1024),
    )(jnp.asarray(hilbert_table()), received)

    part = part.reshape(CORES, PART, lanes)
    mine = lax.dynamic_index_in_dim(part, core, 0, keepdims=False)
    other = lax.dynamic_index_in_dim(part, 1 - core, 0, keepdims=False)
    swap = [(i, i ^ 1) for i in range(Y * X * CORES)]
    summed = mine + lax.ppermute(other, "pair", swap)

    width = 4 * FREQS
    tiles = jnp.zeros((Y, PART, width), jnp.float32)
    for t in range(Z):
        piece = lax.dynamic_slice_in_dim(summed, (my_y + t) % Z * width, width, 1)
        got = lax.ppermute(
            piece,
            ("pair", "grow"),
            [
                (place(y, xc, z), place(z, xc, (y + t) % Z))
                for y in range(Y)
                for xc in range(X * CORES)
                for z in range(Z)
            ],
        )
        tiles = lax.dynamic_update_index_in_dim(tiles, got, (my_z - t) % Z, 0)
    return tiles.reshape(Y * PART, 4, FREQS).transpose(2, 1, 0)


def solution(mesh):
    placed = (P("pair", ("grow", "gcol")), P("pair", ("gcol", "grow")), P("pair"), P("pair"))
    return jax.shard_map(
        per_device,
        mesh=mesh,
        in_specs=placed,
        out_specs=P(None, "grow", ("gcol", "pair")),
        check_vma=False,
    )
```

```python
import functools

import jax
import jax.numpy as jnp
import numpy as np
from jax import lax
from jax.experimental import pallas as pl
from jax.experimental.pallas import tpu as pltpu
from jax.sharding import PartitionSpec as P

BINS = 128
FREQS = 64
GR = 16
Y = 4
X = 4
CORES = 2
Z = 4
CHIPS = Y * X
PART = 48
COLS = CORES * PART
META = GR + 8
STEP = 4
BF16 = jnp.bfloat16
F32 = jnp.float32


def hilbert_table():
    energies = (np.arange(BINS, dtype=np.float32) + np.float32(0.5)) * np.float32(4.0 / BINS)
    real_freq = (np.arange(FREQS, dtype=np.float32) + np.float32(0.5)) * np.float32(4.0 / FREQS)
    broadening = np.float32(4.0 / BINS)
    below = real_freq[:, None] - energies[None, :]
    above = real_freq[:, None] + energies[None, :]
    return below / (below * below + broadening * broadening) - above / (
        above * above + broadening * broadening
    )


def split_table():
    table = hilbert_table()
    high = table.astype(jnp.bfloat16)
    low = (table - high.astype(np.float32)).astype(jnp.bfloat16)
    return np.block([[high, high], [low, low]])


def polarize(groups, table_ref, recv_ref, out_ref, sums_ref):
    pairs = recv_ref.shape[2]
    bin_of_row = lax.broadcasted_iota(jnp.int32, (BINS, pairs), 0).astype(F32)
    for first in range(0, CHIPS, STEP):
        hots = []
        for source in range(first, first + STEP):
            bins = recv_ref[source, COLS + GR : COLS + META, :].astype(F32)[0:1, :]
            hots.append(jnp.where(bins == bin_of_row, 1.0, 0.0).astype(BF16))
        for place, group in enumerate(groups):
            total = None
            for source, hot in enumerate(hots, first):
                slab = recv_ref[source, COLS : COLS + GR, :]
                left = jnp.concatenate(
                    [hot * slab[row : row + 1, :] for row in range(4 * group, 4 * group + 4)],
                    axis=0,
                )
                term = lax.dot_general(
                    left,
                    recv_ref[source, :COLS, :],
                    (((1,), (1,)), ((), ())),
                    preferred_element_type=F32,
                )
                total = term if total is None else total + term
            rows = slice(place * 4 * BINS, (place + 1) * 4 * BINS)
            if first == 0:
                sums_ref[rows, :] = total
            else:
                sums_ref[rows, :] += total
    table = table_ref[...]
    for duo in range(2 * len(groups)):
        both = []
        for row in (2 * duo, 2 * duo + 1):
            spectral = sums_ref[row * BINS : (row + 1) * BINS, :]
            high = spectral.astype(BF16)
            low = (spectral - high.astype(F32)).astype(BF16)
            out = jnp.dot(
                table, jnp.concatenate([high, low], axis=0), preferred_element_type=F32
            )
            both.append(out[:FREQS] + out[FREQS:])
        lane = duo % 2 * 2 * FREQS
        out_ref[duo // 2, :, lane : lane + 2 * FREQS] = jnp.concatenate(both, axis=0).T


def polarize_groups(groups, received):
    rows = len(groups) * 4 * BINS
    return pl.pallas_call(
        functools.partial(polarize, groups),
        out_shape=jax.ShapeDtypeStruct((len(groups), COLS, 4 * FREQS), F32),
        scratch_shapes=[pltpu.VMEM((rows, COLS), F32)],
        compiler_params=pltpu.CompilerParams(vmem_limit_bytes=40 * 1024 * 1024),
        cost_estimate=pl.CostEstimate(
            flops=2 * rows * COLS * received.shape[0] * received.shape[2],
            bytes_accessed=2 * received.size,
            transcendentals=0,
        ),
    )(jnp.asarray(split_table()), received)


def per_device(slab_density, column_density, bin_index, occupation):
    pairs = slab_density.shape[0]
    me = lax.axis_index("pair")
    core = me % CORES
    my_z = lax.axis_index("grow")

    signed = (slab_density * occupation[:, None].astype(BF16)).T
    slabs = lax.all_to_all(
        jnp.broadcast_to(signed[None], (GR // 2, 2, pairs)), ("grow", "gcol"), 0, 0, tiled=True
    ).reshape(Z, 4, pairs)

    twice = jnp.concatenate([slabs, slabs, slabs], axis=0)
    turned = jnp.stack(
        [lax.dynamic_slice_in_dim(twice, y + 2 * core, Z, 0) for y in range(Y)]
    ).reshape(Y, GR, pairs)
    bins = jnp.broadcast_to(bin_index.astype(BF16)[None, None, :], (Y, META - GR, pairs))
    meta = jnp.concatenate([turned, bins], axis=1)
    meta = jnp.broadcast_to(meta[:, None], (Y, X, META, pairs)).reshape(CHIPS, META, pairs)

    columns = column_density.T.reshape(X, CORES, Y, PART, pairs)
    columns = columns.transpose(2, 0, 1, 3, 4).reshape(CHIPS, COLS, pairs)
    received = lax.all_to_all(
        jnp.concatenate([columns, meta], axis=1),
        "pair",
        0,
        0,
        axis_index_groups=[
            [(y * X + x) * CORES + c for y in range(Y) for x in range(X)] for c in range(CORES)
        ],
        tiled=True,
    )

    swap = [(i, i ^ 1) for i in range(Y * X * CORES)]
    theirs = lax.ppermute(polarize_groups((2, 3), received), "pair", swap)
    summed = polarize_groups((0, 1), received) + theirs

    arrived = []
    for t in range(2):
        arrived.append(
            lax.ppermute(
                summed[t],
                ("pair", "grow"),
                [
                    (
                        ((y * X + x) * CORES + c) * Z + z,
                        ((z * X + x) * CORES + c) * Z + (y + 2 * c + t) % Z,
                    )
                    for y in range(Y)
                    for x in range(X)
                    for c in range(CORES)
                    for z in range(Z)
                ],
            )
        )
    arrived = jnp.stack(arrived).reshape(2, CORES, PART, 4 * FREQS)
    keep = lax.dynamic_index_in_dim(arrived, core, 1, keepdims=False)
    give = lax.dynamic_index_in_dim(arrived, 1 - core, 1, keepdims=False)
    got = lax.ppermute(give, "pair", swap)
    tiles = jnp.zeros((Y, PART, 4 * FREQS), F32)
    for t in range(2):
        tiles = lax.dynamic_update_index_in_dim(tiles, keep[t], (my_z - 2 * core - t) % Z, 0)
        tiles = lax.dynamic_update_index_in_dim(
            tiles, got[t], (my_z - 2 * (1 - core) - t) % Z, 0
        )
    return tiles.reshape(Y * PART, 4, FREQS).transpose(2, 1, 0)


def solution(mesh):
    placed = (P("pair", ("grow", "gcol")), P("pair", ("gcol", "grow")), P("pair"), P("pair"))
    return jax.shard_map(
        per_device,
        mesh=mesh,
        in_specs=placed,
        out_specs=P(None, "grow", ("gcol", "pair")),
        check_vma=False,
    )
```

```python
import functools

import jax
import jax.numpy as jnp
import numpy as np
from jax import lax
from jax.experimental import pallas as pl
from jax.experimental.pallas import tpu as pltpu
from jax.sharding import PartitionSpec as P

BINS = 128
FREQS = 64
GR = 16
Y = 4
X = 4
CORES = 2
Z = 4
CHIPS = Y * X
COLS = 96
META = GR + 8
STEP = 4
BF16 = jnp.bfloat16
F32 = jnp.float32


def hilbert_table():
    energies = (np.arange(BINS, dtype=np.float32) + np.float32(0.5)) * np.float32(4.0 / BINS)
    real_freq = (np.arange(FREQS, dtype=np.float32) + np.float32(0.5)) * np.float32(4.0 / FREQS)
    broadening = np.float32(4.0 / BINS)
    below = real_freq[:, None] - energies[None, :]
    above = real_freq[:, None] + energies[None, :]
    return below / (below * below + broadening * broadening) - above / (
        above * above + broadening * broadening
    )


def split_table():
    table = hilbert_table()
    high = table.astype(jnp.bfloat16)
    low = (table - high.astype(np.float32)).astype(jnp.bfloat16)
    return np.block([[high, high], [low, low]])


def polarize(groups, table_ref, recv_ref, out_ref, sums_ref):
    pairs = recv_ref.shape[2]
    bin_of_row = lax.broadcasted_iota(jnp.int32, (BINS, pairs), 0).astype(F32)
    for first in range(0, CHIPS, STEP):
        hots = []
        for source in range(first, first + STEP):
            bins = recv_ref[source, COLS + GR : COLS + META, :].astype(F32)[0:1, :]
            hots.append(jnp.where(bins == bin_of_row, 1.0, 0.0).astype(BF16))
        for place, group in enumerate(groups):
            total = None
            for source, hot in enumerate(hots, first):
                slab = recv_ref[source, COLS : COLS + GR, :]
                left = jnp.concatenate(
                    [hot * slab[row : row + 1, :] for row in range(4 * group, 4 * group + 4)],
                    axis=0,
                )
                term = lax.dot_general(
                    left,
                    recv_ref[source, :COLS, :],
                    (((1,), (1,)), ((), ())),
                    preferred_element_type=F32,
                )
                total = term if total is None else total + term
            rows = slice(place * 4 * BINS, (place + 1) * 4 * BINS)
            if first == 0:
                sums_ref[rows, :] = total
            else:
                sums_ref[rows, :] += total
    table = table_ref[...]
    for duo in range(2 * len(groups)):
        both = []
        for row in (2 * duo, 2 * duo + 1):
            spectral = sums_ref[row * BINS : (row + 1) * BINS, :]
            high = spectral.astype(BF16)
            low = (spectral - high.astype(F32)).astype(BF16)
            out = jnp.dot(
                table, jnp.concatenate([high, low], axis=0), preferred_element_type=F32
            )
            both.append(out[:FREQS] + out[FREQS:])
        lane = duo % 2 * 2 * FREQS
        out_ref[duo // 2, :, lane : lane + 2 * FREQS] = jnp.concatenate(both, axis=0).T


def polarize_groups(groups, received):
    rows = len(groups) * 4 * BINS
    return pl.pallas_call(
        functools.partial(polarize, groups),
        out_shape=jax.ShapeDtypeStruct((len(groups), COLS, 4 * FREQS), F32),
        scratch_shapes=[pltpu.VMEM((rows, COLS), F32)],
        compiler_params=pltpu.CompilerParams(vmem_limit_bytes=40 * 1024 * 1024),
        cost_estimate=pl.CostEstimate(
            flops=2 * rows * COLS * received.shape[0] * received.shape[2],
            bytes_accessed=2 * received.size,
            transcendentals=0,
        ),
    )(jnp.asarray(split_table()), received)


def per_device(slab_density, column_density, bin_index, occupation):
    pairs = slab_density.shape[0]
    me = lax.axis_index("pair")
    core = me % CORES
    my_z = lax.axis_index("grow")

    slabs = lax.all_to_all(
        jnp.broadcast_to(slab_density.T[None], (GR // 2, 2, pairs)),
        ("grow", "gcol"),
        0,
        0,
        tiled=True,
    )
    slabs = slabs.reshape(Z, 4, pairs) * occupation[None, None, :].astype(BF16)

    thrice = jnp.concatenate([slabs, slabs, slabs], axis=0)
    turned = jnp.stack(
        [lax.dynamic_slice_in_dim(thrice, 4 + 2 * core - y, Z, 0) for y in range(Y)]
    ).reshape(Y, GR, pairs)
    bins = jnp.broadcast_to(bin_index.astype(BF16)[None, None, :], (Y, META - GR, pairs))
    meta = jnp.concatenate([turned, bins], axis=1)
    meta = jnp.broadcast_to(meta[:, None], (Y, X, META, pairs)).reshape(CHIPS, META, pairs)

    columns = column_density.T.reshape(X, Y, COLS, pairs)
    columns = columns.transpose(1, 0, 2, 3).reshape(CHIPS, COLS, pairs)
    received = lax.all_to_all(
        jnp.concatenate([columns, meta], axis=1),
        "pair",
        0,
        0,
        axis_index_groups=[
            [(y * X + x) * CORES + c for y in range(Y) for x in range(X)] for c in range(CORES)
        ],
        tiled=True,
    )

    swap = [(i, i ^ 1) for i in range(Y * X * CORES)]
    theirs = lax.ppermute(polarize_groups((2, 3), received), "pair", swap)
    summed = polarize_groups((0, 1), received) + theirs

    arrived = []
    for t in range(2):
        arrived.append(
            lax.ppermute(
                summed[t],
                ("pair", "grow"),
                [
                    (
                        ((y * X + x) * CORES + c) * Z + z,
                        ((z * X + x) * CORES + y // 2) * Z + (2 * c + t - y) % Z,
                    )
                    for y in range(Y)
                    for x in range(X)
                    for c in range(CORES)
                    for z in range(Z)
                ],
            )
        )
    tiles = jnp.where(
        my_z % 2 == 0,
        jnp.concatenate(arrived, axis=0),
        jnp.concatenate(arrived[::-1], axis=0),
    )
    return tiles.reshape(CORES * COLS, 4, FREQS).transpose(2, 1, 0)


def solution(mesh):
    placed = (P("pair", ("grow", "gcol")), P("pair", ("gcol", "grow")), P("pair"), P("pair"))
    return jax.shard_map(
        per_device,
        mesh=mesh,
        in_specs=placed,
        out_specs=P(None, "grow", ("gcol", "pair")),
        check_vma=False,
    )
```

```python
import functools

import jax
import jax.numpy as jnp
import numpy as np
from jax import lax
from jax.experimental import pallas as pl
from jax.experimental.pallas import tpu as pltpu
from jax.sharding import PartitionSpec as P

BINS = 128
FREQS = 64
GR = 16
Y = 4
X = 4
CORES = 2
Z = 4
CHIPS = Y * X
COLS = 96
META = GR + 8
STEP = 4
DISTANCE = (
    ((1, 3), (0, 2)),
    ((0, 2), (1, 3)),
    ((2, 1), (3, 0)),
    ((2, 1), (3, 0)),
)
HALVES = ((0, 3), (1, 2))
BF16 = jnp.bfloat16
F32 = jnp.float32


def hilbert_table():
    energies = (np.arange(BINS, dtype=np.float32) + np.float32(0.5)) * np.float32(4.0 / BINS)
    real_freq = (np.arange(FREQS, dtype=np.float32) + np.float32(0.5)) * np.float32(4.0 / FREQS)
    broadening = np.float32(4.0 / BINS)
    below = real_freq[:, None] - energies[None, :]
    above = real_freq[:, None] + energies[None, :]
    return below / (below * below + broadening * broadening) - above / (
        above * above + broadening * broadening
    )


def split_table():
    table = hilbert_table()
    high = table.astype(jnp.bfloat16)
    low = (table - high.astype(np.float32)).astype(jnp.bfloat16)
    return np.block([[high, high], [low, low]])


def polarize(groups, table_ref, recv_ref, out_ref, sums_ref):
    pairs = recv_ref.shape[2]
    bin_of_row = lax.broadcasted_iota(jnp.int32, (BINS, pairs), 0).astype(F32)
    for first in range(0, CHIPS, STEP):
        hots = []
        for source in range(first, first + STEP):
            bins = recv_ref[source, COLS + GR : COLS + META, :].astype(F32)[0:1, :]
            hots.append(jnp.where(bins == bin_of_row, 1.0, 0.0).astype(BF16))
        for place, group in enumerate(groups):
            total = None
            for source, hot in enumerate(hots, first):
                slab = recv_ref[source, COLS : COLS + GR, :]
                left = jnp.concatenate(
                    [hot * slab[row : row + 1, :] for row in range(4 * group, 4 * group + 4)],
                    axis=0,
                )
                term = lax.dot_general(
                    left,
                    recv_ref[source, :COLS, :],
                    (((1,), (1,)), ((), ())),
                    preferred_element_type=F32,
                )
                total = term if total is None else total + term
            rows = slice(place * 4 * BINS, (place + 1) * 4 * BINS)
            if first == 0:
                sums_ref[rows, :] = total
            else:
                sums_ref[rows, :] += total
    table = table_ref[...]
    for duo in range(2 * len(groups)):
        both = []
        for row in (2 * duo, 2 * duo + 1):
            spectral = sums_ref[row * BINS : (row + 1) * BINS, :]
            high = spectral.astype(BF16)
            low = (spectral - high.astype(F32)).astype(BF16)
            out = jnp.dot(
                table, jnp.concatenate([high, low], axis=0), preferred_element_type=F32
            )
            both.append(out[:FREQS] + out[FREQS:])
        lane = duo % 2 * 2 * FREQS
        out_ref[duo // 2, :, lane : lane + 2 * FREQS] = jnp.concatenate(both, axis=0).T


def polarize_groups(groups, received):
    rows = len(groups) * 4 * BINS
    return pl.pallas_call(
        functools.partial(polarize, groups),
        out_shape=jax.ShapeDtypeStruct((len(groups), COLS, 4 * FREQS), F32),
        scratch_shapes=[pltpu.VMEM((rows, COLS), F32)],
        compiler_params=pltpu.CompilerParams(vmem_limit_bytes=40 * 1024 * 1024),
        cost_estimate=pl.CostEstimate(
            flops=2 * rows * COLS * received.shape[0] * received.shape[2],
            bytes_accessed=2 * received.size,
            transcendentals=0,
        ),
    )(jnp.asarray(split_table()), received)


def per_device(slab_density, column_density, bin_index, occupation):
    pairs = slab_density.shape[0]
    me = lax.axis_index("pair")
    core = me % CORES
    my_y = me // (X * CORES)
    my_z = lax.axis_index("grow")

    slabs = lax.all_to_all(
        jnp.broadcast_to(slab_density.T[None], (GR // 2, 2, pairs)),
        ("grow", "gcol"),
        0,
        0,
        tiled=True,
    )
    slabs = slabs.reshape(Z, 4, pairs) * occupation[None, None, :].astype(BF16)

    slabs = lax.dynamic_slice_in_dim(jnp.concatenate([slabs, slabs], axis=0), my_z, Z, 0)
    bins = jnp.broadcast_to(bin_index.astype(BF16)[None, :], (META - GR, pairs))
    columns = column_density.T.reshape(X, Y, COLS, pairs)
    payload = []
    for step in range(Y):
        keep, give = DISTANCE[step]
        meta = jnp.where(
            core == 0,
            jnp.concatenate([slabs[i] for i in keep + give] + [bins], axis=0),
            jnp.concatenate([slabs[i] for i in give + keep] + [bins], axis=0),
        )
        part = next(2 * c + HALVES[c].index(step) for c in range(CORES) if step in HALVES[c])
        payload.append(
            jnp.concatenate([columns[:, part], jnp.broadcast_to(meta[None], (X, META, pairs))], axis=1)
        )
    payload = lax.dynamic_slice_in_dim(jnp.stack(payload + payload), (Y - my_z) % Y, Y, 0)
    received = lax.all_to_all(
        payload.reshape(CHIPS, COLS + META, pairs),
        "pair",
        0,
        0,
        axis_index_groups=[
            [(y * X + x) * CORES + c for y in range(Y) for x in range(X)] for c in range(CORES)
        ],
        tiled=True,
    )

    swap = [(i, i ^ 1) for i in range(Y * X * CORES)]
    theirs = lax.ppermute(polarize_groups((2, 3), received), "pair", swap)
    summed = polarize_groups((0, 1), received) + theirs

    arrived = []
    for t in range(2):
        moves = []
        for y in range(Y):
            for z in range(Z):
                step = (y - z) % Y
                to_core = 0 if step in HALVES[0] else 1
                for x in range(X):
                    for c in range(CORES):
                        source = ((y * X + x) * CORES + c) * Z + z
                        target = ((z * X + x) * CORES + to_core) * Z
                        moves.append((source, target + (z + DISTANCE[step][c][t]) % Z))
        arrived.append(lax.ppermute(summed[t], ("pair", "grow"), moves))
    first = np.zeros((CORES, Z), np.int32)
    for c in range(CORES):
        for half in range(2):
            for group in DISTANCE[HALVES[c][half]]:
                first[c, group[0]] = half
    my_first = jnp.asarray(first.reshape(-1))[core * Z + (my_z - my_y) % Z]
    tiles = jnp.where(
        my_first == 0,
        jnp.concatenate(arrived, axis=0),
        jnp.concatenate(arrived[::-1], axis=0),
    )
    return tiles.reshape(CORES * COLS, 4, FREQS).transpose(2, 1, 0)


def solution(mesh):
    placed = (P("pair", ("grow", "gcol")), P("pair", ("gcol", "grow")), P("pair"), P("pair"))
    return jax.shard_map(
        per_device,
        mesh=mesh,
        in_specs=placed,
        out_specs=P(None, "grow", ("gcol", "pair")),
        check_vma=False,
    )
```

```python
import functools

import jax
import jax.numpy as jnp
import numpy as np
from jax import lax
from jax.experimental import pallas as pl
from jax.experimental.pallas import tpu as pltpu
from jax.sharding import PartitionSpec as P

BINS = 128
FREQS = 64
GR = 16
Y = 4
X = 4
CORES = 2
Z = 4
CHIPS = Y * X
COLS = 96
META = GR + 8
STEP = 4
DISTANCE = (
    ((1, 3), (0, 2)),
    ((0, 2), (1, 3)),
    ((2, 1), (3, 0)),
    ((2, 1), (3, 0)),
)
HALVES = ((0, 3), (1, 2))
ORDER = ((2, 3), (1, 2), (1, 3), (1, 1), (2, 0), (3, 3), (0, 2), (3, 2), (0, 3), (2, 1), (3, 1), (1, 0), (3, 0), (0, 1), (2, 2), (0, 0))
BF16 = jnp.bfloat16
F32 = jnp.float32


def hilbert_table():
    energies = (np.arange(BINS, dtype=np.float32) + np.float32(0.5)) * np.float32(4.0 / BINS)
    real_freq = (np.arange(FREQS, dtype=np.float32) + np.float32(0.5)) * np.float32(4.0 / FREQS)
    broadening = np.float32(4.0 / BINS)
    below = real_freq[:, None] - energies[None, :]
    above = real_freq[:, None] + energies[None, :]
    return below / (below * below + broadening * broadening) - above / (
        above * above + broadening * broadening
    )


def split_table():
    table = hilbert_table()
    high = table.astype(jnp.bfloat16)
    low = (table - high.astype(np.float32)).astype(jnp.bfloat16)
    return np.block([[high, high], [low, low]])


def polarize(groups, table_ref, recv_ref, out_ref, sums_ref):
    pairs = recv_ref.shape[2]
    bin_of_row = lax.broadcasted_iota(jnp.int32, (BINS, pairs), 0).astype(F32)
    for first in range(0, CHIPS, STEP):
        hots = []
        for source in range(first, first + STEP):
            bins = recv_ref[source, COLS + GR : COLS + META, :].astype(F32)[0:1, :]
            hots.append(jnp.where(bins == bin_of_row, 1.0, 0.0).astype(BF16))
        for place, group in enumerate(groups):
            total = None
            for source, hot in enumerate(hots, first):
                slab = recv_ref[source, COLS : COLS + GR, :]
                left = jnp.concatenate(
                    [hot * slab[row : row + 1, :] for row in range(4 * group, 4 * group + 4)],
                    axis=0,
                )
                term = lax.dot_general(
                    left,
                    recv_ref[source, :COLS, :],
                    (((1,), (1,)), ((), ())),
                    preferred_element_type=F32,
                )
                total = term if total is None else total + term
            rows = slice(place * 4 * BINS, (place + 1) * 4 * BINS)
            if first == 0:
                sums_ref[rows, :] = total
            else:
                sums_ref[rows, :] += total
    table = table_ref[...]
    for duo in range(2 * len(groups)):
        both = []
        for row in (2 * duo, 2 * duo + 1):
            spectral = sums_ref[row * BINS : (row + 1) * BINS, :]
            high = spectral.astype(BF16)
            low = (spectral - high.astype(F32)).astype(BF16)
            out = jnp.dot(
                table, jnp.concatenate([high, low], axis=0), preferred_element_type=F32
            )
            both.append(out[:FREQS] + out[FREQS:])
        lane = duo % 2 * 2 * FREQS
        out_ref[duo // 2, :, lane : lane + 2 * FREQS] = jnp.concatenate(both, axis=0).T


def polarize_groups(groups, received):
    rows = len(groups) * 4 * BINS
    return pl.pallas_call(
        functools.partial(polarize, groups),
        out_shape=jax.ShapeDtypeStruct((len(groups), COLS, 4 * FREQS), F32),
        scratch_shapes=[pltpu.VMEM((rows, COLS), F32)],
        compiler_params=pltpu.CompilerParams(vmem_limit_bytes=40 * 1024 * 1024),
        cost_estimate=pl.CostEstimate(
            flops=2 * rows * COLS * received.shape[0] * received.shape[2],
            bytes_accessed=2 * received.size,
            transcendentals=0,
        ),
    )(jnp.asarray(split_table()), received)


def per_device(slab_density, column_density, bin_index, occupation):
    pairs = slab_density.shape[0]
    me = lax.axis_index("pair")
    core = me % CORES
    my_y = me // (X * CORES)
    my_z = lax.axis_index("grow")

    slabs = lax.all_to_all(
        jnp.broadcast_to(slab_density.T[None], (GR // 2, 2, pairs)),
        ("grow", "gcol"),
        0,
        0,
        tiled=True,
    )
    slabs = slabs.reshape(Z, 4, pairs) * occupation[None, None, :].astype(BF16)

    slabs = lax.dynamic_slice_in_dim(jnp.concatenate([slabs, slabs], axis=0), my_z, Z, 0)
    bins = jnp.broadcast_to(bin_index.astype(BF16)[None, :], (META - GR, pairs))
    columns = column_density.T.reshape(X, Y, COLS, pairs)
    payload = []
    for step in range(Y):
        keep, give = DISTANCE[step]
        meta = jnp.where(
            core == 0,
            jnp.concatenate([slabs[i] for i in keep + give] + [bins], axis=0),
            jnp.concatenate([slabs[i] for i in give + keep] + [bins], axis=0),
        )
        part = next(2 * c + HALVES[c].index(step) for c in range(CORES) if step in HALVES[c])
        payload.append(
            jnp.concatenate([columns[:, part], jnp.broadcast_to(meta[None], (X, META, pairs))], axis=1)
        )
    payload = lax.dynamic_slice_in_dim(jnp.stack(payload + payload), (Y - my_z) % Y, Y, 0)
    received = lax.all_to_all(
        jnp.stack([payload[y, x] for y, x in ORDER]),
        "pair",
        0,
        0,
        axis_index_groups=[
            [(y * X + x) * CORES + c for y, x in ORDER] for c in range(CORES)
        ],
        tiled=True,
    )

    swap = [(i, i ^ 1) for i in range(Y * X * CORES)]
    theirs = lax.ppermute(polarize_groups((2, 3), received), "pair", swap)
    summed = polarize_groups((0, 1), received) + theirs

    arrived = []
    for t in range(2):
        moves = []
        for y in range(Y):
            for z in range(Z):
                step = (y - z) % Y
                to_core = 0 if step in HALVES[0] else 1
                for x in range(X):
                    for c in range(CORES):
                        source = ((y * X + x) * CORES + c) * Z + z
                        target = ((z * X + x) * CORES + to_core) * Z
                        moves.append((source, target + (z + DISTANCE[step][c][t]) % Z))
        arrived.append(lax.ppermute(summed[t], ("pair", "grow"), moves))
    first = np.zeros((CORES, Z), np.int32)
    for c in range(CORES):
        for half in range(2):
            for group in DISTANCE[HALVES[c][half]]:
                first[c, group[0]] = half
    my_first = jnp.asarray(first.reshape(-1))[core * Z + (my_z - my_y) % Z]
    tiles = jnp.where(
        my_first == 0,
        jnp.concatenate(arrived, axis=0),
        jnp.concatenate(arrived[::-1], axis=0),
    )
    return tiles.reshape(CORES * COLS, 4, FREQS).transpose(2, 1, 0)


def solution(mesh):
    placed = (P("pair", ("grow", "gcol")), P("pair", ("gcol", "grow")), P("pair"), P("pair"))
    return jax.shard_map(
        per_device,
        mesh=mesh,
        in_specs=placed,
        out_specs=P(None, "grow", ("gcol", "pair")),
        check_vma=False,
    )
```

```python
import functools

import jax
import jax.numpy as jnp
import numpy as np
from jax import lax
from jax.experimental import pallas as pl
from jax.experimental.pallas import tpu as pltpu
from jax.sharding import PartitionSpec as P

BINS = 128
FREQS = 64
GR = 16
Y = 4
X = 4
CORES = 2
Z = 4
CHIPS = Y * X
COLS = 96
LANES = 128
STEP = 4
DISTANCE = (
    ((1, 3), (0, 2)),
    ((0, 3), (2, 1)),
    ((1, 0), (3, 2)),
    ((2, 1), (3, 0)),
)
HALVES = ((0, 3), (1, 2))
ORDER = ((2, 3), (1, 2), (1, 3), (1, 1), (2, 0), (3, 3), (0, 2), (3, 2), (0, 3), (2, 1), (3, 1), (1, 0), (3, 0), (0, 1), (2, 2), (0, 0))
BF16 = jnp.bfloat16
F32 = jnp.float32


def hilbert_table():
    energies = (np.arange(BINS, dtype=np.float32) + np.float32(0.5)) * np.float32(4.0 / BINS)
    real_freq = (np.arange(FREQS, dtype=np.float32) + np.float32(0.5)) * np.float32(4.0 / FREQS)
    broadening = np.float32(4.0 / BINS)
    below = real_freq[:, None] - energies[None, :]
    above = real_freq[:, None] + energies[None, :]
    return below / (below * below + broadening * broadening) - above / (
        above * above + broadening * broadening
    )


def split_table():
    table = hilbert_table()
    high = table.astype(jnp.bfloat16)
    low = (table - high.astype(np.float32)).astype(jnp.bfloat16)
    return np.block([[high, high], [low, low]])


def polarize(groups, table_ref, recv_ref, out_ref, sums_ref):
    pairs = 2 * LANES

    def both_halves(source, first, rows):
        return jnp.concatenate(
            [recv_ref[source, first + half * rows : first + (half + 1) * rows, :] for half in (0, 1)],
            axis=1,
        )

    bin_of_row = lax.broadcasted_iota(jnp.int32, (BINS, pairs), 0).astype(F32)
    for first in range(0, CHIPS, STEP):
        hots = []
        for source in range(first, first + STEP):
            bins = recv_ref[source, 2 * (COLS + GR) :, :].astype(F32)
            bins = jnp.concatenate([bins[0:1, :], bins[1:2, :]], axis=1)
            hots.append(jnp.where(bins == bin_of_row, 1.0, 0.0).astype(BF16))
        for place, group in enumerate(groups):
            total = None
            for source, hot in enumerate(hots, first):
                slab = both_halves(source, 2 * COLS, GR)
                left = jnp.concatenate(
                    [hot * slab[row : row + 1, :] for row in range(4 * group, 4 * group + 4)],
                    axis=0,
                )
                term = lax.dot_general(
                    left,
                    both_halves(source, 0, COLS),
                    (((1,), (1,)), ((), ())),
                    preferred_element_type=F32,
                )
                total = term if total is None else total + term
            rows = slice(place * 4 * BINS, (place + 1) * 4 * BINS)
            if first == 0:
                sums_ref[rows, :] = total
            else:
                sums_ref[rows, :] += total
    table = table_ref[...]
    for duo in range(2 * len(groups)):
        both = []
        for row in (2 * duo, 2 * duo + 1):
            spectral = sums_ref[row * BINS : (row + 1) * BINS, :]
            high = spectral.astype(BF16)
            low = (spectral - high.astype(F32)).astype(BF16)
            out = jnp.dot(
                table, jnp.concatenate([high, low], axis=0), preferred_element_type=F32
            )
            both.append(out[:FREQS] + out[FREQS:])
        lane = duo % 2 * 2 * FREQS
        out_ref[duo // 2, :, lane : lane + 2 * FREQS] = jnp.concatenate(both, axis=0).T


def polarize_groups(groups, received):
    rows = len(groups) * 4 * BINS
    return pl.pallas_call(
        functools.partial(polarize, groups),
        out_shape=jax.ShapeDtypeStruct((len(groups), COLS, 4 * FREQS), F32),
        scratch_shapes=[pltpu.VMEM((rows, COLS), F32)],
        compiler_params=pltpu.CompilerParams(vmem_limit_bytes=40 * 1024 * 1024),
        cost_estimate=pl.CostEstimate(
            flops=2 * rows * COLS * received.shape[0] * 2 * LANES,
            bytes_accessed=2 * received.size,
            transcendentals=0,
        ),
    )(jnp.asarray(split_table()), received)


def per_device(slab_density, column_density, bin_index, occupation):
    pairs = slab_density.shape[0]
    me = lax.axis_index("pair")
    core = me % CORES
    my_y = me // (X * CORES)
    my_z = lax.axis_index("grow")

    slabs = lax.all_to_all(
        jnp.broadcast_to(slab_density.T[None], (GR // 2, 2, pairs)),
        ("grow", "gcol"),
        0,
        0,
        tiled=True,
    )
    slabs = slabs.reshape(Z, 4, pairs) * occupation[None, None, :].astype(BF16)

    codes = [0, 0]
    for step in range(Y):
        for c in range(CORES):
            for place, group in enumerate(DISTANCE[step][c] + DISTANCE[step][1 - c]):
                codes[c] |= group << (2 * (Z * step + place))
    ys = sum(y << (2 * i) for i, (y, _) in enumerate(ORDER))
    code = jnp.where(core == 0, np.uint32(codes[0]), np.uint32(codes[1]))
    z = my_z.astype(jnp.uint32)
    shape = (CHIPS, Z, 1, 1)
    chip = lax.broadcasted_iota(jnp.uint32, shape, 0)
    place = lax.broadcasted_iota(jnp.uint32, shape, 1)
    step = ((np.uint32(ys) >> (2 * chip)) + Z - z) % Z
    group = ((code >> (2 * (Z * step + place))) + z) % Z
    meta = slabs[0]
    for i in range(1, Z):
        meta = jnp.where(group == i, slabs[i], meta)
    meta = meta.reshape(CHIPS, GR, pairs)
    meta = jnp.concatenate([meta[..., :LANES], meta[..., LANES:]], axis=1)
    bins = jnp.pad(bin_index.astype(BF16).reshape(2, LANES), ((0, 6), (0, 0)))
    bins = jnp.broadcast_to(bins[None], (CHIPS, 8, LANES))

    columns = column_density.T.reshape(X, Y, COLS, pairs)
    columns = jnp.concatenate([columns[..., :LANES], columns[..., LANES:]], axis=2)
    parts = [2 * c + HALVES[c].index(o) for o in range(Y) for c in range(CORES) if o in HALVES[c]]
    columns = jnp.stack([columns[:, part] for part in parts + parts])
    columns = lax.dynamic_slice_in_dim(columns, (Y - my_z) % Y, Y, 0)
    columns = jnp.stack([columns[y, x] for y, x in ORDER])
    received = lax.all_to_all(
        jnp.concatenate([columns, meta, bins], axis=1),
        "pair",
        0,
        0,
        axis_index_groups=[
            [(y * X + x) * CORES + c for y, x in ORDER] for c in range(CORES)
        ],
        tiled=True,
    )

    swap = [(i, i ^ 1) for i in range(Y * X * CORES)]
    theirs = lax.ppermute(polarize_groups((2, 3), received), "pair", swap)
    summed = polarize_groups((0, 1), received) + theirs

    arrived = []
    for t in range(2):
        moves = []
        for y in range(Y):
            for z in range(Z):
                step = (y - z) % Y
                to_core = 0 if step in HALVES[0] else 1
                for x in range(X):
                    for c in range(CORES):
                        source = ((y * X + x) * CORES + c) * Z + z
                        target = ((z * X + x) * CORES + to_core) * Z
                        moves.append((source, target + (z + DISTANCE[step][c][t]) % Z))
        arrived.append(lax.ppermute(summed[t], ("pair", "grow"), moves))
    first = 0
    for c in range(CORES):
        for half, step in enumerate(HALVES[c]):
            for group in DISTANCE[step]:
                first |= half << (Z * c + group[0])
    my_first = (first >> (Z * core + (my_z - my_y) % Z)) & 1
    tiles = jnp.where(
        my_first == 0,
        jnp.concatenate(arrived, axis=0),
        jnp.concatenate(arrived[::-1], axis=0),
    )
    return tiles.reshape(CORES * COLS, 4, FREQS).transpose(2, 1, 0)


def solution(mesh):
    placed = (P("pair", ("grow", "gcol")), P("pair", ("gcol", "grow")), P("pair"), P("pair"))
    return jax.shard_map(
        per_device,
        mesh=mesh,
        in_specs=placed,
        out_specs=P(None, "grow", ("gcol", "pair")),
        check_vma=False,
    )
```

```python
import functools

import jax
import jax.numpy as jnp
import numpy as np
from jax import lax
from jax.experimental import pallas as pl
from jax.experimental.pallas import tpu as pltpu
from jax.sharding import PartitionSpec as P

BINS = 128
FREQS = 64
GR = 16
Y = 4
X = 4
CORES = 2
Z = 4
CHIPS = Y * X
COLS = 96
LANES = 128
STEP = 4
DISTANCE = (
    ((1, 3), (0, 2)),
    ((0, 3), (2, 1)),
    ((1, 0), (3, 2)),
    ((2, 1), (3, 0)),
)
HALVES = ((0, 3), (1, 2))
ORDER = ((2, 2), (3, 3), (0, 2), (3, 2), (0, 1), (2, 1), (1, 3), (2, 3), (1, 1), (3, 0), (2, 0), (3, 1), (0, 3), (1, 0), (0, 0), (1, 2))
BF16 = jnp.bfloat16
F32 = jnp.float32


def hilbert_table():
    energies = (np.arange(BINS, dtype=np.float32) + np.float32(0.5)) * np.float32(4.0 / BINS)
    real_freq = (np.arange(FREQS, dtype=np.float32) + np.float32(0.5)) * np.float32(4.0 / FREQS)
    broadening = np.float32(4.0 / BINS)
    below = real_freq[:, None] - energies[None, :]
    above = real_freq[:, None] + energies[None, :]
    return below / (below * below + broadening * broadening) - above / (
        above * above + broadening * broadening
    )


def split_table():
    table = hilbert_table()
    high = table.astype(jnp.bfloat16)
    low = (table - high.astype(np.float32)).astype(jnp.bfloat16)
    return np.block([[high, high], [low, low]])


def polarize(groups, table_ref, bins_ref, recv_ref, out_ref, sums_ref):
    pairs = 2 * LANES

    def both_halves(source, first, rows):
        return jnp.concatenate(
            [recv_ref[source, first + half * rows : first + (half + 1) * rows, :] for half in (0, 1)],
            axis=1,
        )

    bin_of_row = lax.broadcasted_iota(jnp.int32, (BINS, pairs), 0).astype(F32)
    for first in range(0, CHIPS, STEP):
        hots = []
        for source in range(first, first + STEP):
            bins = bins_ref[source : source + 1, :]
            hots.append(jnp.where(bins == bin_of_row, 1.0, 0.0).astype(BF16))
        for place, group in enumerate(groups):
            total = None
            for source, hot in enumerate(hots, first):
                slab = both_halves(source, 2 * COLS, GR)
                left = jnp.concatenate(
                    [hot * slab[row : row + 1, :] for row in range(4 * group, 4 * group + 4)],
                    axis=0,
                )
                term = lax.dot_general(
                    left,
                    both_halves(source, 0, COLS),
                    (((1,), (1,)), ((), ())),
                    preferred_element_type=F32,
                )
                total = term if total is None else total + term
            rows = slice(place * 4 * BINS, (place + 1) * 4 * BINS)
            if first == 0:
                sums_ref[rows, :] = total
            else:
                sums_ref[rows, :] += total
    table = table_ref[...]
    for duo in range(2 * len(groups)):
        both = []
        for row in (2 * duo, 2 * duo + 1):
            spectral = sums_ref[row * BINS : (row + 1) * BINS, :]
            high = spectral.astype(BF16)
            low = (spectral - high.astype(F32)).astype(BF16)
            out = jnp.dot(
                table, jnp.concatenate([high, low], axis=0), preferred_element_type=F32
            )
            both.append(out[:FREQS] + out[FREQS:])
        lane = duo % 2 * 2 * FREQS
        out_ref[duo // 2, :, lane : lane + 2 * FREQS] = jnp.concatenate(both, axis=0).T


def polarize_groups(groups, bins, received):
    rows = len(groups) * 4 * BINS
    return pl.pallas_call(
        functools.partial(polarize, groups),
        out_shape=jax.ShapeDtypeStruct((len(groups), COLS, 4 * FREQS), F32),
        scratch_shapes=[pltpu.VMEM((rows, COLS), F32)],
        compiler_params=pltpu.CompilerParams(vmem_limit_bytes=40 * 1024 * 1024),
        cost_estimate=pl.CostEstimate(
            flops=2 * rows * COLS * received.shape[0] * 2 * LANES,
            bytes_accessed=2 * received.size,
            transcendentals=0,
        ),
    )(jnp.asarray(split_table()), bins, received)


def per_device(slab_density, column_density, bin_index, occupation):
    pairs = slab_density.shape[0]
    me = lax.axis_index("pair")
    core = me % CORES
    my_y = me // (X * CORES)
    my_z = lax.axis_index("grow")

    slabs = lax.all_to_all(
        jnp.broadcast_to(slab_density.T[None], (GR // 2, 2, pairs)),
        ("grow", "gcol"),
        0,
        0,
        tiled=True,
    )
    slabs = slabs.reshape(Z, 4, pairs) * occupation[None, None, :].astype(BF16)

    codes = [0, 0]
    for step in range(Y):
        for c in range(CORES):
            for place, group in enumerate(DISTANCE[step][c] + DISTANCE[step][1 - c]):
                codes[c] |= group << (2 * (Z * step + place))
    ys = sum(y << (2 * i) for i, (y, _) in enumerate(ORDER))
    code = jnp.where(core == 0, np.uint32(codes[0]), np.uint32(codes[1]))
    z = my_z.astype(jnp.uint32)
    shape = (CHIPS, Z, 1, 1)
    chip = lax.broadcasted_iota(jnp.uint32, shape, 0)
    place = lax.broadcasted_iota(jnp.uint32, shape, 1)
    step = ((np.uint32(ys) >> (2 * chip)) + Z - z) % Z
    group = ((code >> (2 * (Z * step + place))) + z) % Z
    meta = slabs[0]
    for i in range(1, Z):
        meta = jnp.where(group == i, slabs[i], meta)
    meta = meta.reshape(CHIPS, GR, pairs)
    meta = jnp.concatenate([meta[..., :LANES], meta[..., LANES:]], axis=1)
    bins = jnp.pad(bin_index.astype(BF16).reshape(2, LANES), ((0, 6), (0, 0)))
    bins = jnp.broadcast_to(bins[None], (CHIPS, 8, LANES))

    columns = column_density.T.reshape(X, Y, COLS, pairs)
    columns = jnp.concatenate([columns[..., :LANES], columns[..., LANES:]], axis=2)
    parts = [2 * c + HALVES[c].index(o) for o in range(Y) for c in range(CORES) if o in HALVES[c]]
    columns = jnp.stack([columns[:, part] for part in parts + parts])
    columns = lax.dynamic_slice_in_dim(columns, (Y - my_z) % Y, Y, 0)
    columns = jnp.stack([columns[y, x] for y, x in ORDER])
    received = lax.all_to_all(
        jnp.concatenate([columns, meta, bins], axis=1),
        "pair",
        0,
        0,
        axis_index_groups=[
            [(y * X + x) * CORES + c for y, x in ORDER] for c in range(CORES)
        ],
        tiled=True,
    )

    bins = received[:, 2 * (COLS + GR) :][:, :2].reshape(CHIPS, pairs).astype(F32)
    received = received[:, : 2 * (COLS + GR)]
    swap = [(i, i ^ 1) for i in range(Y * X * CORES)]
    theirs = lax.ppermute(polarize_groups((2, 3), bins, received), "pair", swap)
    summed = polarize_groups((0, 1), bins, received) + theirs

    arrived = []
    for t in range(2):
        moves = []
        for y in range(Y):
            for z in range(Z):
                step = (y - z) % Y
                to_core = 0 if step in HALVES[0] else 1
                for x in range(X):
                    for c in range(CORES):
                        source = ((y * X + x) * CORES + c) * Z + z
                        target = ((z * X + x) * CORES + to_core) * Z
                        moves.append((source, target + (z + DISTANCE[step][c][t]) % Z))
        arrived.append(lax.ppermute(summed[t], ("pair", "grow"), moves))
    first = 0
    for c in range(CORES):
        for half, step in enumerate(HALVES[c]):
            for group in DISTANCE[step]:
                first |= half << (Z * c + group[0])
    my_first = (first >> (Z * core + (my_z - my_y) % Z)) & 1
    tiles = jnp.where(
        my_first == 0,
        jnp.concatenate(arrived, axis=0),
        jnp.concatenate(arrived[::-1], axis=0),
    )
    return tiles.reshape(CORES * COLS, 4, FREQS).transpose(2, 1, 0)


def solution(mesh):
    placed = (P("pair", ("grow", "gcol")), P("pair", ("gcol", "grow")), P("pair"), P("pair"))
    return jax.shard_map(
        per_device,
        mesh=mesh,
        in_specs=placed,
        out_specs=P(None, "grow", ("gcol", "pair")),
        check_vma=False,
    )
```

```python
import functools

import jax
import jax.numpy as jnp
import numpy as np
from jax import lax
from jax.experimental import pallas as pl
from jax.experimental.pallas import tpu as pltpu
from jax.sharding import PartitionSpec as P

BINS = 128
FREQS = 64
GR = 16
Y = 4
X = 4
CORES = 2
Z = 4
CHIPS = Y * X
COLS = 96
LANES = 128
STEP = 4
DISTANCE = (
    ((1, 3), (0, 2)),
    ((0, 3), (2, 1)),
    ((1, 0), (3, 2)),
    ((2, 1), (3, 0)),
)
HALVES = ((0, 3), (1, 2))
ORDER = ((2, 2), (3, 3), (0, 2), (3, 2), (0, 1), (2, 1), (1, 3), (2, 3), (1, 1), (3, 0), (2, 0), (3, 1), (0, 3), (1, 0), (0, 0), (1, 2))
BF16 = jnp.bfloat16
F32 = jnp.float32


def hilbert_table():
    energies = (np.arange(BINS, dtype=np.float32) + np.float32(0.5)) * np.float32(4.0 / BINS)
    real_freq = (np.arange(FREQS, dtype=np.float32) + np.float32(0.5)) * np.float32(4.0 / FREQS)
    broadening = np.float32(4.0 / BINS)
    below = real_freq[:, None] - energies[None, :]
    above = real_freq[:, None] + energies[None, :]
    return below / (below * below + broadening * broadening) - above / (
        above * above + broadening * broadening
    )


def split_table():
    table = hilbert_table()
    high = table.astype(jnp.bfloat16)
    low = (table - high.astype(np.float32)).astype(jnp.bfloat16)
    return np.block([[high, high], [low, low]])


def polarize(groups, table_ref, bins_ref, recv_ref, out_ref, sums_ref):
    pairs = 2 * LANES

    def both_halves(source, first, rows):
        return jnp.concatenate(
            [recv_ref[source, first + half * rows : first + (half + 1) * rows, :] for half in (0, 1)],
            axis=1,
        )

    bin_of_row = lax.broadcasted_iota(jnp.int32, (BINS, pairs), 0).astype(F32)
    for first in range(0, CHIPS, STEP):
        hots = []
        for source in range(first, first + STEP):
            bins = bins_ref[source : source + 1, :]
            hots.append(jnp.where(bins == bin_of_row, 1.0, 0.0).astype(BF16))
        for place, group in enumerate(groups):
            total = None
            for source, hot in enumerate(hots, first):
                slab = both_halves(source, 2 * COLS, GR)
                left = jnp.concatenate(
                    [hot * slab[row : row + 1, :] for row in range(4 * group, 4 * group + 4)],
                    axis=0,
                )
                term = lax.dot_general(
                    left,
                    both_halves(source, 0, COLS),
                    (((1,), (1,)), ((), ())),
                    preferred_element_type=F32,
                )
                total = term if total is None else total + term
            rows = slice(place * 4 * BINS, (place + 1) * 4 * BINS)
            if first == 0:
                sums_ref[rows, :] = total
            else:
                sums_ref[rows, :] += total
    table = table_ref[...]
    for duo in range(2 * len(groups)):
        both = []
        for row in (2 * duo, 2 * duo + 1):
            spectral = sums_ref[row * BINS : (row + 1) * BINS, :]
            high = spectral.astype(BF16)
            low = (spectral - high.astype(F32)).astype(BF16)
            out = jnp.dot(
                table, jnp.concatenate([high, low], axis=0), preferred_element_type=F32
            )
            both.append(out[:FREQS] + out[FREQS:])
        lane = duo % 2 * 2 * FREQS
        out_ref[duo // 2, :, lane : lane + 2 * FREQS] = jnp.concatenate(both, axis=0).T


def polarize_groups(groups, bins, received):
    rows = len(groups) * 4 * BINS
    return pl.pallas_call(
        functools.partial(polarize, groups),
        out_shape=jax.ShapeDtypeStruct((len(groups), COLS, 4 * FREQS), F32),
        scratch_shapes=[pltpu.VMEM((rows, COLS), F32)],
        compiler_params=pltpu.CompilerParams(vmem_limit_bytes=40 * 1024 * 1024),
        cost_estimate=pl.CostEstimate(
            flops=2 * rows * COLS * received.shape[0] * 2 * LANES,
            bytes_accessed=2 * received.size,
            transcendentals=0,
        ),
    )(jnp.asarray(split_table()), bins, received)


def per_device(slab_density, column_density, bin_index, occupation):
    pairs = slab_density.shape[0]
    me = lax.axis_index("pair")
    core = me % CORES
    my_y = me // (X * CORES)
    my_z = lax.axis_index("grow")

    slabs = lax.all_to_all(
        jnp.broadcast_to(slab_density.T[None], (GR // 2, 2, pairs)),
        ("grow", "gcol"),
        0,
        0,
        tiled=True,
    )
    slabs = slabs.reshape(Z, 4, pairs) * occupation[None, None, :].astype(BF16)

    codes = [0, 0]
    for step in range(Y):
        for c in range(CORES):
            for place, group in enumerate(DISTANCE[step][c] + DISTANCE[step][1 - c]):
                codes[c] |= group << (2 * (Z * step + place))
    ys = sum(y << (2 * i) for i, (y, _) in enumerate(ORDER))
    code = jnp.where(core == 0, np.uint32(codes[0]), np.uint32(codes[1]))
    z = my_z.astype(jnp.uint32)
    shape = (CHIPS, Z, 1, 1)
    chip = lax.broadcasted_iota(jnp.uint32, shape, 0)
    place = lax.broadcasted_iota(jnp.uint32, shape, 1)
    step = ((np.uint32(ys) >> (2 * chip)) + Z - z) % Z
    group = ((code >> (2 * (Z * step + place))) + z) % Z
    meta = slabs[0]
    for i in range(1, Z):
        meta = jnp.where(group == i, slabs[i], meta)
    meta = meta.reshape(CHIPS, GR, pairs)
    meta = jnp.concatenate([meta[..., :LANES], meta[..., LANES:]], axis=1)
    bins = jnp.pad(bin_index.astype(BF16).reshape(2, LANES), ((0, 6), (0, 0)))
    bins = jnp.broadcast_to(bins[None], (CHIPS, 8, LANES))

    columns = column_density.T.reshape(X, Y, COLS, pairs)
    columns = jnp.concatenate([columns[..., :LANES], columns[..., LANES:]], axis=2)
    parts = [2 * c + HALVES[c].index(o) for o in range(Y) for c in range(CORES) if o in HALVES[c]]
    columns = jnp.stack([columns[:, part] for part in parts + parts])
    columns = lax.dynamic_slice_in_dim(columns, (Y - my_z) % Y, Y, 0)
    columns = jnp.stack([columns[y, x] for y, x in ORDER])
    received = lax.all_to_all(
        jnp.concatenate([columns, meta, bins], axis=1),
        "pair",
        0,
        0,
        axis_index_groups=[
            [(y * X + x) * CORES + c for y, x in ORDER] for c in range(CORES)
        ],
        tiled=True,
    )

    bins = received[:, 2 * (COLS + GR) :][:, :2].reshape(CHIPS, pairs).astype(F32)
    swap = [(i, i ^ 1) for i in range(Y * X * CORES)]
    theirs = lax.ppermute(polarize_groups((2, 3), bins, received), "pair", swap)
    summed = polarize_groups((0, 1), bins, received) + theirs

    arrived = []
    for t in range(2):
        moves = []
        for y in range(Y):
            for z in range(Z):
                step = (y - z) % Y
                to_core = 0 if step in HALVES[0] else 1
                for x in range(X):
                    for c in range(CORES):
                        source = ((y * X + x) * CORES + c) * Z + z
                        target = ((z * X + x) * CORES + to_core) * Z
                        moves.append((source, target + (z + DISTANCE[step][c][t]) % Z))
        arrived.append(lax.ppermute(summed[t], ("pair", "grow"), moves))
    first = 0
    for c in range(CORES):
        for half, step in enumerate(HALVES[c]):
            for group in DISTANCE[step]:
                first |= half << (Z * c + group[0])
    my_first = (first >> (Z * core + (my_z - my_y) % Z)) & 1
    tiles = jnp.where(
        my_first == 0,
        jnp.concatenate(arrived, axis=0),
        jnp.concatenate(arrived[::-1], axis=0),
    )
    return tiles.reshape(CORES * COLS, 4, FREQS).transpose(2, 1, 0)


def solution(mesh):
    placed = (P("pair", ("grow", "gcol")), P("pair", ("gcol", "grow")), P("pair"), P("pair"))
    return jax.shard_map(
        per_device,
        mesh=mesh,
        in_specs=placed,
        out_specs=P(None, "grow", ("gcol", "pair")),
        check_vma=False,
    )
```
